1024 devices in a mesh: gx: 64 (over z, y), gy: 16 (over x, core).
Axes of the slice: x: 8, y: 8, z: 8, core: 2. Of those that a mesh axis runs over, the one named last changes fastest.
Arguments:
- tokens: bfloat16 [128, 16384], P('gy', 'gx'), may hold values from -6 to 6
- gate_weight: bfloat16 [16384, 32768], P('gx', 'gy'), may hold values from -0.046875 to 0.046875
- up_weight: bfloat16 [16384, 32768], P('gx', 'gy'), may hold values from -0.046875 to 0.046875
- gate_scale: float32 [32768], P('gy'), may hold values from 0.1 to 1.9
- up_scale: float32 [32768], P('gy'), may hold values from 0.1 to 1.9
- down_weight: bfloat16 [32768, 16384], P('gy', 'gx'), may hold values from -0.03125 to 0.03125
- down_scale: float32 [16384], P('gx'), may hold values from 0.1 to 1.9
Outputs:
- result: bfloat16 [128, 16384], P('gy', 'gx')
The draws below stay inside these ranges and needn't reach their ends.
All inputs are finite; a program needn't handle non-finite values.
Results may differ from the reference program's by a relative error of at most 0.011.
Values may be sent and summed in bfloat16 or wider, within the bound.
A program may use at most 32 MiB of HBM per device.

```python
import jax
import jax.numpy as jnp

D = 16384
FF = 32768
TOKENS = 128


def block_scale(rng, shape, split, low, top_value):
    def one(axis_at, shards_of):
        draws = jax.random.uniform(jax.random.fold_in(jax.random.fold_in(rng, 6), axis_at), (shards_of,), jnp.float32, low / len(split), top_value / len(split))
        return jnp.repeat(jnp.exp(draws), shape[axis_at] // shards_of).reshape((-1,) + (1,) * (len(shape) - axis_at - 1))

    factor_of = one(*split[0])
    for cut in split[1:]:
        factor_of = factor_of * one(*cut)
    return factor_of


def gaussian(key, extent, scale, limit, shards=(), dtype=jnp.bfloat16):
    gain = block_scale(key, extent, shards, -0.22, 0.18) if shards else 1.0
    drawn = jax.random.normal(key, extent, jnp.float32) * scale * gain
    return jnp.minimum(jnp.maximum(drawn, -limit), limit).astype(dtype)


def setup_inputs(seed: int = 0) -> dict:
    splits = jax.random.split(jax.random.key(seed), 8)
    return {
        "tokens": gaussian(splits[0], (TOKENS, D), 1.0, 6.0, ((0, 16), (1, 64))),
        "gate_weight": gaussian(splits[1], (D, FF), D ** -0.5, 0.046875, ((0, 64), (1, 16))),
        "up_weight": gaussian(splits[2], (D, FF), D ** -0.5, 0.046875, ((0, 64), (1, 16))),
        "gate_scale": jnp.clip(1.0 + 0.18 * jax.random.normal(splits[3], (FF,), jnp.float32), 0.1, 1.9),
        "up_scale": jnp.clip(1.0 + 0.18 * jax.random.normal(splits[4], (FF,), jnp.float32), 0.1, 1.9),
        "down_weight": gaussian(splits[5], (FF, D), FF ** -0.5, 0.03125, ((0, 16), (1, 64))),
        "down_scale": jnp.clip(1.0 + 0.18 * jax.random.normal(splits[6], (D,), jnp.float32), 0.1, 1.9),
    }


def reference(tokens, gate_weight, up_weight, gate_scale, up_scale, down_weight, down_scale):
    gate_act = jnp.dot(tokens, gate_weight, preferred_element_type=jnp.float32) * gate_scale
    up_act = jnp.dot(tokens, up_weight, preferred_element_type=jnp.float32) * up_scale
    hidden = (jax.nn.silu(gate_act) * up_act).astype(jnp.bfloat16)
    summed = jnp.dot(hidden, down_weight, preferred_element_type=jnp.float32)
    return (summed * down_scale).astype(jnp.bfloat16)
```

```python
import functools

import jax
import jax.numpy as jnp
from jax import lax
from jax.experimental import pallas as pl
from jax.experimental.pallas import tpu as pltpu
from jax.sharding import PartitionSpec as P

MESH = pl.DeviceIdType.MESH
F32, BF16 = jnp.float32, jnp.bfloat16


def far_first(n):
    return sorted(range(1, n), key=lambda d: -min(d, n - d))


def near_first(n):
    return far_first(n)[::-1]


def kernel(n, m, tokens_hbm, gate_hbm, up_hbm, gate_scale_hbm, up_scale_hbm, down_hbm, down_scale_hbm, out_ref,
           tokens_own, gate_w, up_w, gate_s, up_s, down_w, down_s,
           packed, gathered, part, got1, total, sums1, got2, hidden, last, got3,
           load_sem, tok_send, tok_recv, r1_send, r1_recv, r2_send, r2_recv, g1_send, g1_recv, g2_send, g2_recv, f_send, f_recv):
    gx, gy = lax.axis_index("gx"), lax.axis_index("gy")
    z, y = gx // n, lax.rem(gx, n)
    half = 128 * n

    def along(axis, d):
        if axis == 0:
            return (z * n + lax.rem(y + d, n), gy)
        return (lax.rem(z + d, n) * n + y, gy)

    def along_gy(d):
        return (gx, lax.rem(gy + d, m))

    def where(axis, d):
        return lax.rem((y if axis == 0 else z) + d, n)

    def copy(src, dst, send, recv, to):
        return pltpu.make_async_remote_copy(
            src_ref=src, dst_ref=dst, send_sem=send, recv_sem=recv, device_id=to, device_id_type=MESH
        )

    loads = [
        pltpu.make_async_copy(a, b, load_sem.at[i])
        for i, (a, b) in enumerate(
            (
                (tokens_hbm, tokens_own),
                (gate_hbm, gate_w),
                (up_hbm, up_w),
                (gate_scale_hbm, gate_s),
                (up_scale_hbm, up_s),
                (down_hbm, down_w),
                (down_scale_hbm, down_s),
            )
        )
    ]
    for load in loads:
        load.start()

    barrier = pltpu.get_barrier_semaphore()
    for d in range(1, m):
        pl.semaphore_signal(barrier, inc=1, device_id=along_gy(d), device_id_type=MESH)
    for axis in (0, 1):
        for d in range(1, n):
            pl.semaphore_signal(barrier, inc=1, device_id=along(axis, d), device_id_type=MESH)

    loads[0].wait()
    own = tokens_own[...].astype(F32)
    packed[...] = jnp.concatenate([own[:, :128], own[:, 128:]], axis=0).astype(BF16)
    gathered[gy] = packed[...]
    pl.semaphore_wait(barrier, m - 1 + 2 * (n - 1))

    sends = []

    def start(c):
        c.start()
        sends.append(c)

    order = sorted(range(1, m), key=lambda d: -min(d // 2, n - d // 2))
    for d in order:
        start(copy(packed, gathered.at[gy], tok_send.at[d - 1], tok_recv.at[d - 1], along_gy(d)))
    for d in order[::-1]:
        copy(packed, gathered.at[lax.rem(gy + m - d, m)], tok_send.at[d - 1], tok_recv.at[d - 1], along_gy(d)).wait_recv()
    wide = gathered[...].astype(F32)
    x = jnp.concatenate([wide[:, :8].reshape(8 * m, 128), wide[:, 8:].reshape(8 * m, 128)], axis=1).astype(BF16)

    loads[1].wait()
    loads[2].wait()
    for h in (0, 1):
        cols = slice(h * half, (h + 1) * half)
        part[h, :, :, :half] = jnp.dot(x, gate_w[:, cols], preferred_element_type=F32).astype(BF16).reshape(n, 16, half)
        part[h, :, :, half:] = jnp.dot(x, up_w[:, cols], preferred_element_type=F32).astype(BF16).reshape(n, 16, half)
        for d in far_first(n):
            start(copy(part.at[h, where(h, d)], got1.at[h, d - 1], r1_send.at[h, d - 1], r1_recv.at[h, d - 1], along(h, d)))
    for h in (0, 1):
        total[h] = part[h, where(h, 0)].astype(F32)
    order = near_first(n)
    for d in order[:-1]:
        for h in (0, 1):
            copy(part.at[h, 0], got1.at[h, d - 1], r1_send.at[h, d - 1], r1_recv.at[h, d - 1], along(h, d)).wait_recv()
            total[h] += got1[h, d - 1].astype(F32)
    d = order[-1]
    for h in (0, 1):
        copy(part.at[h, 0], got1.at[h, d - 1], r1_send.at[h, d - 1], r1_recv.at[h, d - 1], along(h, d)).wait_recv()
        done = total[h] + got1[h, d - 1].astype(F32)
        for j in range(n):
            sums1[h, j, :, :128] = done[:, j * 128 : j * 128 + 128].astype(BF16)
            sums1[h, j, :, 128:] = done[:, half + j * 128 : half + j * 128 + 128].astype(BF16)
        for e in far_first(n):
            start(copy(sums1.at[h, where(1 - h, e)], got2.at[h, e - 1], r2_send.at[h, e - 1], r2_recv.at[h, e - 1], along(1 - h, e)))

    loads[3].wait()
    loads[4].wait()
    for h in (0, 1):
        i, j = where(h, 0), where(1 - h, 0)
        acc = sums1[h, j].astype(F32)
        for e in near_first(n):
            copy(sums1.at[h, 0], got2.at[h, e - 1], r2_send.at[h, e - 1], r2_recv.at[h, e - 1], along(1 - h, e)).wait_recv()
            acc += got2[h, e - 1].astype(F32)
        gate = acc[:, :128] * gate_s[pl.ds(h * n + j, 1), :]
        up = acc[:, 128:] * up_s[pl.ds(h * n + j, 1), :]
        mine = pl.ds(pl.multiple_of(j * 128, 128), 128)
        hidden[h, i, :, mine] = (gate / (1.0 + jnp.exp(-gate)) * up).astype(BF16)
        for e in far_first(n):
            spot = hidden.at[h, i, :, mine]
            start(copy(spot, spot, g1_send.at[h, e - 1], g1_recv.at[h, e - 1], along(1 - h, e)))
    for h in (0, 1):
        i, j = where(h, 0), where(1 - h, 0)
        for e in near_first(n):
            spot = hidden.at[h, i, :, pl.ds(pl.multiple_of(where(1 - h, n - e) * 128, 128), 128)]
            copy(spot, spot, g1_send.at[h, e - 1], g1_recv.at[h, e - 1], along(1 - h, e)).wait_recv()
        for d in far_first(n):
            spot = hidden.at[h, i]
            start(copy(spot, spot, g2_send.at[h, d - 1], g2_recv.at[h, d - 1], along(h, d)))
    loads[5].wait()
    for h in (0, 1):
        for d in near_first(n):
            spot = hidden.at[h, where(h, n - d)]
            copy(spot, spot, g2_send.at[h, d - 1], g2_recv.at[h, d - 1], along(h, d)).wait_recv()
    result = jnp.dot(hidden[0].reshape(8 * m, half), down_w[:half, :], preferred_element_type=F32)
    result += jnp.dot(hidden[1].reshape(8 * m, half), down_w[half:, :], preferred_element_type=F32)

    pieces = result.reshape(m, 8, 256)
    last[...] = jnp.concatenate([pieces[:, :, :128], pieces[:, :, 128:]], axis=1).astype(BF16)
    order = sorted(range(1, m), key=lambda d: -min(d // 2, n - d // 2))
    for d in order:
        start(copy(last.at[lax.rem(gy + d, m)], got3.at[d - 1], f_send.at[d - 1], f_recv.at[d - 1], along_gy(d)))
    loads[6].wait()
    acc = last[gy].astype(F32)
    for d in order[::-1]:
        copy(last.at[0], got3.at[d - 1], f_send.at[d - 1], f_recv.at[d - 1], along_gy(d)).wait_recv()
        acc += got3[d - 1].astype(F32)
    out_ref[...] = (jnp.concatenate([acc[:8], acc[8:]], axis=1) * down_s[...]).astype(BF16)
    for c in sends:
        c.wait_send()


def solution(mesh):
    n = int(round(mesh.shape["gx"] ** 0.5))
    m = mesh.shape["gy"]
    half = 128 * n
    dma = pltpu.SemaphoreType.DMA

    def local(tokens, gate_weight, up_weight, gate_scale, up_scale, down_weight, down_scale):
        return pl.pallas_call(
            functools.partial(kernel, n, m),
            out_shape=jax.ShapeDtypeStruct((8, 256), BF16),
            in_specs=[pl.BlockSpec(memory_space=pltpu.HBM)] * 7,
            out_specs=pl.BlockSpec(memory_space=pltpu.VMEM),
            scratch_shapes=[
                pltpu.VMEM((8, 256), BF16),
                pltpu.VMEM((256, 2 * half), BF16),
                pltpu.VMEM((256, 2 * half), BF16),
                pltpu.VMEM((2 * n, 128), F32),
                pltpu.VMEM((2 * n, 128), F32),
                pltpu.VMEM((2 * half, 256), BF16),
                pltpu.VMEM((1, 256), F32),
                pltpu.VMEM((16, 128), BF16),
                pltpu.VMEM((m, 16, 128), BF16),
                pltpu.VMEM((2, n, 16, 2 * half), BF16),
                pltpu.VMEM((2, n - 1, 16, 2 * half), BF16),
                pltpu.VMEM((2, 16, 2 * half), F32),
                pltpu.VMEM((2, n, 16, 256), BF16),
                pltpu.VMEM((2, n - 1, 16, 256), BF16),
                pltpu.VMEM((2, n, 16, half), BF16),
                pltpu.VMEM((m, 16, 128), BF16),
                pltpu.VMEM((m - 1, 16, 128), BF16),
                dma((7,)),
                dma((m - 1,)),
                dma((m - 1,)),
                *([dma((2, n - 1))] * 8),
                dma((m - 1,)),
                dma((m - 1,)),
            ],
            compiler_params=pltpu.CompilerParams(
                collective_id=0, has_side_effects=True, vmem_limit_bytes=60 << 20
            ),
            name="feed_forward",
        )(
            tokens,
            gate_weight,
            up_weight,
            gate_scale.reshape(2 * n, 128),
            up_scale.reshape(2 * n, 128),
            down_weight,
            down_scale.reshape(1, 256),
        )

    return jax.shard_map(
        local,
        mesh=mesh,
        in_specs=(P("gy", "gx"), P("gx", "gy"), P("gx", "gy"), P("gy"), P("gy"), P("gy", "gx"), P("gx")),
        out_specs=P("gy", "gx"),
        check_vma=False,
    )
```

```python
import functools

import jax
import jax.numpy as jnp
from jax import lax
from jax.experimental import pallas as pl
from jax.experimental.pallas import tpu as pltpu
from jax.sharding import PartitionSpec as P

MESH = pl.DeviceIdType.MESH
F32, BF16 = jnp.float32, jnp.bfloat16


def far_first(n):
    return sorted(range(1, n), key=lambda d: -min(d, n - d))


def cut(n, parts):
    return [(n * k // parts, n * (k + 1) // parts) for k in range(parts)]


CHUNKS = 3
GROUPS = 3


def kernel(n, m, chunks, groups, tokens_hbm, gate_hbm, up_hbm, gate_scale_hbm, up_scale_hbm, down_hbm, down_scale_hbm, out_ref,
           tokens_own, weights, gate_s, up_s, down_w, down_s, packed, gathered, *rest):
    parts, rest = rest[: len(chunks)], rest[len(chunks) :]
    got1, rest = rest[: len(chunks)], rest[len(chunks) :]
    sums1, got2 = rest[:2]
    hidden, rest = rest[2 : 2 + len(groups)], rest[2 + len(groups) :]
    last, got3, load_sem, tok_sem, r1_sem, r2_sem, g1_sem, g2_sem, f_sem = rest
    gx, gy = lax.axis_index("gx"), lax.axis_index("gy")
    z, y = gx // n, lax.rem(gx, n)
    to_send = far_first(n) + [0]
    to_keep = to_send[::-1]

    def place(q):
        for g, (a, b) in enumerate(groups):
            if a <= q < b:
                return g, q - a

    def along(axis, d):
        if axis == 0:
            return (z * n + lax.rem(y + d, n), gy)
        return (lax.rem(z + d, n) * n + y, gy)

    def along_gy(d):
        return (gx, lax.rem(gy + d, m))

    def where(axis, d):
        return lax.rem((y if axis == 0 else z) + d, n)

    def send(src, dst, sems, to):
        pltpu.make_async_remote_copy(
            src_ref=src, dst_ref=dst, send_sem=sems.at[0], recv_sem=sems.at[1], device_id=to, device_id_type=MESH
        ).start()

    def wait(sem, like):
        pltpu.make_async_copy(like, like, sem).wait()

    barrier = pltpu.get_barrier_semaphore()
    load_tokens = pltpu.make_async_copy(tokens_hbm, tokens_own, load_sem.at[0])
    load_tokens.start()
    by_distance = sorted(range(1, m), key=lambda d: -min(d // 2, n - d // 2))
    for d in by_distance:
        pl.semaphore_signal(barrier, inc=1, device_id=along_gy(d), device_id_type=MESH)
    for d in far_first(n):
        for axis in (0, 1):
            pl.semaphore_signal(barrier, inc=1, device_id=along(axis, d), device_id_type=MESH)

    for h in (0, 1):
        for p, e in enumerate(to_send):
            block = pl.ds(pl.multiple_of((h * n + where(1 - h, e)) * 128, 128), 128)
            pltpu.make_async_copy(gate_hbm.at[:, block], weights.at[h, :, pl.ds(p * 256, 128)], load_sem.at[1]).start()
            pltpu.make_async_copy(up_hbm.at[:, block], weights.at[h, :, pl.ds(p * 256 + 128, 128)], load_sem.at[1]).start()

    load_tokens.wait()
    own = tokens_own[...].astype(F32)
    packed[...] = jnp.concatenate([own[:, :128], own[:, 128:]], axis=0).astype(BF16)
    gathered[gy] = packed[...]
    pl.semaphore_wait(barrier, m - 1 + 2 * (n - 1))
    for d in by_distance:
        send(packed, gathered.at[gy], tok_sem, along_gy(d))
    for h in (0, 1):
        for q, e in enumerate(to_keep):
            block = pl.ds(pl.multiple_of((h * n + where(1 - h, e)) * 128, 128), 128)
            pltpu.make_async_copy(down_hbm.at[block, :], down_w.at[pl.ds((h * n + q) * 128, 128), :], load_sem.at[2]).start()
    small = [
        pltpu.make_async_copy(a, b, load_sem.at[3 + k])
        for k, (a, b) in enumerate(((gate_scale_hbm, gate_s), (up_scale_hbm, up_s), (down_scale_hbm, down_s)))
    ]
    for load in small:
        load.start()
    wait(load_sem.at[1], weights)
    wait(tok_sem.at[1], gathered.at[pl.ds(0, m - 1)])
    wide = gathered[...].astype(F32)
    x = jnp.concatenate([wide[:, :8].reshape(8 * m, 128), wide[:, 8:].reshape(8 * m, 128)], axis=1).astype(BF16)

    for c, (a, b) in enumerate(chunks):
        for h in (0, 1):
            sums = jnp.dot(x, weights[h, :, a * 256 : b * 256], preferred_element_type=F32)
            parts[c][h] = sums.astype(BF16).reshape(n, 16, (b - a) * 256)
            for d in far_first(n):
                send(parts[c].at[h, where(h, d)], got1[c].at[h, d - 1], r1_sem.at[h, c], along(h, d))
    wait(tok_sem.at[0], gathered.at[pl.ds(0, m - 1)])
    for load in small:
        load.wait()
    wait(load_sem.at[2], down_w)
    for c, (a, b) in enumerate(chunks):
        for h in (0, 1):
            wait(r1_sem.at[h, c, 1], got1[c].at[h])
            acc = parts[c][h, where(h, 0)].astype(F32)
            for d in range(1, n):
                acc += got1[c][h, d - 1].astype(F32)
            for p in range(a, b):
                sums1[h, p] = acc[:, (p - a) * 256 : (p - a + 1) * 256].astype(BF16)
            for p in range(a, b):
                if to_send[p]:
                    send(sums1.at[h, p], got2.at[h, p], r2_sem.at[h], along(1 - h, to_send[p]))

    for c in range(len(chunks)):
        for h in (0, 1):
            wait(r1_sem.at[h, c, 0], got1[c].at[h])
    for h in (0, 1):
        i, j = where(h, 0), where(1 - h, 0)
        wait(r2_sem.at[h, 1], got2.at[h])
        acc = sums1[h, n - 1].astype(F32)
        for p in range(n - 1):
            acc += got2[h, p].astype(F32)
        gate = acc[:, :128] * gate_s[pl.ds(h * n + j, 1), :]
        up = acc[:, 128:] * up_s[pl.ds(h * n + j, 1), :]
        hidden[0][h, i, 0] = (gate / (1.0 + jnp.exp(-gate)) * up).astype(BF16)
        for f in far_first(n):
            g, k = place(to_keep.index(n - f))
            send(hidden[0].at[h, i, 0], hidden[g].at[h, i, k], g1_sem.at[h, to_keep.index(n - f)], along(1 - h, f))
    for h in (0, 1):
        wait(r2_sem.at[h, 0], got2.at[h])
    for g, (a, b) in enumerate(groups):
        for h in (0, 1):
            i = where(h, 0)
            for q in range(max(a, 1), b):
                wait(g1_sem.at[h, q, 1], hidden[g].at[h, i, q - a])
            for d in far_first(n):
                send(hidden[g].at[h, i], hidden[g].at[h, i], g2_sem.at[h, g], along(h, d))
    for h in (0, 1):
        for q in range(1, n):
            wait(g1_sem.at[h, q, 0], hidden[0].at[h, 0, 0])
    result = jnp.zeros((8 * m, 256), F32)
    for g, (a, b) in enumerate(groups):
        for h in (0, 1):
            wait(g2_sem.at[h, g, 1], hidden[g].at[h, pl.ds(0, n - 1)])
            left = jnp.concatenate([hidden[g][h, :, k].reshape(8 * m, 128) for k in range(b - a)], axis=1)
            result += jnp.dot(left, down_w[(h * n + a) * 128 : (h * n + b) * 128, :], preferred_element_type=F32)

    pieces = result.reshape(m, 8, 256)
    last[...] = jnp.concatenate([pieces[:, :, :128], pieces[:, :, 128:]], axis=1).astype(BF16)
    for d in by_distance:
        send(last.at[lax.rem(gy + d, m)], got3.at[d - 1], f_sem, along_gy(d))
    for g in range(len(groups)):
        for h in (0, 1):
            wait(g2_sem.at[h, g, 0], hidden[g].at[h, pl.ds(0, n - 1)])
    acc = last[gy].astype(F32)
    wait(f_sem.at[1], got3)
    acc += jnp.sum(got3[...].astype(F32), axis=0)
    out_ref[...] = (jnp.concatenate([acc[:8], acc[8:]], axis=1) * down_s[...]).astype(BF16)
    wait(f_sem.at[0], got3)


def solution(mesh):
    n = int(round(mesh.shape["gx"] ** 0.5))
    m = mesh.shape["gy"]
    chunks, groups = cut(n, CHUNKS), cut(n, GROUPS)
    half = 128 * n
    dma = pltpu.SemaphoreType.DMA

    def local(tokens, gate_weight, up_weight, gate_scale, up_scale, down_weight, down_scale):
        return pl.pallas_call(
            functools.partial(kernel, n, m, chunks, groups),
            out_shape=jax.ShapeDtypeStruct((8, 256), BF16),
            in_specs=[pl.BlockSpec(memory_space=pltpu.HBM)] * 7,
            out_specs=pl.BlockSpec(memory_space=pltpu.VMEM),
            scratch_shapes=[
                pltpu.VMEM((8, 256), BF16),
                pltpu.VMEM((2, 256, 2 * half), BF16),
                pltpu.VMEM((2 * n, 128), F32),
                pltpu.VMEM((2 * n, 128), F32),
                pltpu.VMEM((2 * half, 256), BF16),
                pltpu.VMEM((1, 256), F32),
                pltpu.VMEM((16, 128), BF16),
                pltpu.VMEM((m, 16, 128), BF16),
                *[pltpu.VMEM((2, n, 16, (b - a) * 256), BF16) for a, b in chunks],
                *[pltpu.VMEM((2, n - 1, 16, (b - a) * 256), BF16) for a, b in chunks],
                pltpu.VMEM((2, n, 16, 256), BF16),
                pltpu.VMEM((2, n - 1, 16, 256), BF16),
                *[pltpu.VMEM((2, n, b - a, 16, 128), BF16) for a, b in groups],
                pltpu.VMEM((m, 16, 128), BF16),
                pltpu.VMEM((m - 1, 16, 128), BF16),
                dma((6,)),
                dma((2,)),
                dma((2, len(chunks), 2)),
                dma((2, 2)),
                dma((2, n, 2)),
                dma((2, len(groups), 2)),
                dma((2,)),
            ],
            compiler_params=pltpu.CompilerParams(
                collective_id=0, has_side_effects=True, vmem_limit_bytes=60 << 20
            ),
            name="feed_forward",
        )(
            tokens,
            gate_weight,
            up_weight,
            gate_scale.reshape(2 * n, 128),
            up_scale.reshape(2 * n, 128),
            down_weight,
            down_scale.reshape(1, 256),
        )

    return jax.shard_map(
        local,
        mesh=mesh,
        in_specs=(P("gy", "gx"), P("gx", "gy"), P("gx", "gy"), P("gy"), P("gy"), P("gy", "gx"), P("gx")),
        out_specs=P("gy", "gx"),
        check_vma=False,
    )
```

```python
import functools

import jax
import jax.numpy as jnp
from jax import lax
from jax.experimental import pallas as pl
from jax.experimental.pallas import tpu as pltpu
from jax.sharding import PartitionSpec as P

MESH = pl.DeviceIdType.MESH
F32, BF16 = jnp.float32, jnp.bfloat16


def far_first(n):
    return sorted(range(1, n), key=lambda d: -min(d, n - d))


def routes(n):
    if n == 8:
        return [(-4, -2), (-3, -1)], [(3, 1)], [-1, 1]
    return [], [], list(range(1, n))


def cut(n, parts):
    return [(n * k // parts, n * (k + 1) // parts) for k in range(parts)]


CHUNKS = 3
GROUPS = 3


def kernel(n, m, chunks, groups, tokens_hbm, gate_hbm, up_hbm, gate_scale_hbm, up_scale_hbm, down_hbm, down_scale_hbm, out_ref,
           tokens_own, weights, gate_s, up_s, down_w, down_s, packed, gathered, *rest):
    parts, rest = rest[: len(chunks)], rest[len(chunks) :]
    got1, rest = rest[: len(chunks)], rest[len(chunks) :]
    relayed, rest = rest[: len(chunks)], rest[len(chunks) :]
    passed, rest = rest[: len(chunks)], rest[len(chunks) :]
    sums1, got2 = rest[:2]
    hidden, rest = rest[2 : 2 + len(groups)], rest[2 + len(groups) :]
    last, got3, load_sem, tok_sem, rl_sem, r1_sem, r2_sem, g1_sem, g2_sem, f_sem = rest
    gx, gy = lax.axis_index("gx"), lax.axis_index("gy")
    z, y = gx // n, lax.rem(gx, n)
    to_send = far_first(n) + [0]
    to_keep = to_send[::-1]

    def place(q):
        for g, (a, b) in enumerate(groups):
            if a <= q < b:
                return g, q - a

    def along(axis, d):
        if axis == 0:
            return (z * n + lax.rem(y + d, n), gy)
        return (lax.rem(z + d, n) * n + y, gy)

    def along_gy(d):
        return (gx, lax.rem(gy + d, m))

    side = 1 - 2 * lax.rem(gy, 2)

    def turned(d):
        return lax.rem(side * d + 2 * n, n)

    def where(axis, d):
        return lax.rem((y if axis == 0 else z) + d, n)

    def send(src, dst, sems, to):
        pltpu.make_async_remote_copy(
            src_ref=src, dst_ref=dst, send_sem=sems.at[0], recv_sem=sems.at[1], device_id=to, device_id_type=MESH
        ).start()

    def wait(sem, like):
        pltpu.make_async_copy(like, like, sem).wait()

    barrier = pltpu.get_barrier_semaphore()
    load_tokens = pltpu.make_async_copy(tokens_hbm, tokens_own, load_sem.at[0])
    load_tokens.start()
    by_distance = sorted(range(1, m), key=lambda d: -min(d // 2, n - d // 2))
    for d in by_distance:
        pl.semaphore_signal(barrier, inc=1, device_id=along_gy(d), device_id_type=MESH)
    for d in far_first(n):
        for axis in (0, 1):
            pl.semaphore_signal(barrier, inc=1, device_id=along(axis, d), device_id_type=MESH)

    for h in (0, 1):
        for p, e in enumerate(to_send):
            block = pl.ds(pl.multiple_of((h * n + where(1 - h, e)) * 128, 128), 128)
            pltpu.make_async_copy(gate_hbm.at[:, block], weights.at[h, :, pl.ds(p * 256, 128)], load_sem.at[1]).start()
            pltpu.make_async_copy(up_hbm.at[:, block], weights.at[h, :, pl.ds(p * 256 + 128, 128)], load_sem.at[1]).start()

    load_tokens.wait()
    own = tokens_own[...].astype(F32)
    packed[...] = jnp.concatenate([own[:, :128], own[:, 128:]], axis=0).astype(BF16)
    gathered[gy] = packed[...]
    pl.semaphore_wait(barrier, m - 1 + 2 * (n - 1))
    for d in by_distance:
        send(packed, gathered.at[gy], tok_sem, along_gy(d))
    for h in (0, 1):
        for q, e in enumerate(to_keep):
            block = pl.ds(pl.multiple_of((h * n + where(1 - h, e)) * 128, 128), 128)
            pltpu.make_async_copy(down_hbm.at[block, :], down_w.at[pl.ds((h * n + q) * 128, 128), :], load_sem.at[2]).start()
    small = [
        pltpu.make_async_copy(a, b, load_sem.at[3 + k])
        for k, (a, b) in enumerate(((gate_scale_hbm, gate_s), (up_scale_hbm, up_s), (down_scale_hbm, down_s)))
    ]
    for load in small:
        load.start()
    wait(load_sem.at[1], weights)
    wait(tok_sem.at[1], gathered.at[pl.ds(0, m - 1)])
    wide = gathered[...].astype(F32)
    x = jnp.concatenate([wide[:, :8].reshape(8 * m, 128), wide[:, 8:].reshape(8 * m, 128)], axis=1).astype(BF16)

    ahead, behind, direct = routes(n)
    for c, (a, b) in enumerate(chunks):
        for h in (0, 1):
            sums = jnp.dot(x, weights[h, :, a * 256 : b * 256], preferred_element_type=F32)
            parts[c][h] = sums.astype(BF16).reshape(n, 16, (b - a) * 256)
            for s, (far, stop) in enumerate(ahead + behind):
                send(parts[c].at[h, where(h, turned(far))], relayed[c].at[h, s], rl_sem.at[h, c], along(h, turned(stop)))
            for s, d in enumerate(direct):
                send(parts[c].at[h, where(h, turned(d))], got1[c].at[h, s], r1_sem.at[h, c], along(h, turned(d)))
    wait(tok_sem.at[0], gathered.at[pl.ds(0, m - 1)])
    for load in small:
        load.wait()
    wait(load_sem.at[2], down_w)
    for c in range(len(chunks)):
        for h in (0, 1):
            if ahead:
                wait(rl_sem.at[h, c, 1], relayed[c].at[h])
                for s, (d, first, count) in enumerate(((-2, 0, len(ahead)), (2, len(ahead), len(behind)))):
                    acc = parts[c][h, where(h, turned(d))].astype(F32)
                    for k in range(first, first + count):
                        acc += relayed[c][h, k].astype(F32)
                    passed[c][h, s] = acc.astype(BF16)
                    send(passed[c].at[h, s], got1[c].at[h, len(direct) + s], r1_sem.at[h, c], along(h, turned(d)))
    for c, (a, b) in enumerate(chunks):
        for h in (0, 1):
            wait(r1_sem.at[h, c, 1], got1[c].at[h])
            acc = parts[c][h, where(h, 0)].astype(F32)
            for k in range(got1[c].shape[1]):
                acc += got1[c][h, k].astype(F32)
            for p in range(a, b):
                sums1[h, p] = acc[:, (p - a) * 256 : (p - a + 1) * 256].astype(BF16)
            for p in range(a, b):
                if to_send[p]:
                    send(sums1.at[h, p], got2.at[h, p], r2_sem.at[h], along(1 - h, to_send[p]))

    for c in range(len(chunks)):
        for h in (0, 1):
            wait(r1_sem.at[h, c, 0], got1[c].at[h])
            if ahead:
                wait(rl_sem.at[h, c, 0], relayed[c].at[h])
    for h in (0, 1):
        i, j = where(h, 0), where(1 - h, 0)
        wait(r2_sem.at[h, 1], got2.at[h])
        acc = sums1[h, n - 1].astype(F32)
        for p in range(n - 1):
            acc += got2[h, p].astype(F32)
        gate = acc[:, :128] * gate_s[pl.ds(h * n + j, 1), :]
        up = acc[:, 128:] * up_s[pl.ds(h * n + j, 1), :]
        hidden[0][h, i, 0] = (gate / (1.0 + jnp.exp(-gate)) * up).astype(BF16)
        for f in far_first(n):
            g, k = place(to_keep.index(n - f))
            send(hidden[0].at[h, i, 0], hidden[g].at[h, i, k], g1_sem.at[h, to_keep.index(n - f)], along(1 - h, f))
    for h in (0, 1):
        wait(r2_sem.at[h, 0], got2.at[h])
    for g, (a, b) in enumerate(groups):
        for h in (0, 1):
            i = where(h, 0)
            for q in range(max(a, 1), b):
                wait(g1_sem.at[h, q, 1], hidden[g].at[h, i, q - a])
            for d in far_first(n):
                send(hidden[g].at[h, i], hidden[g].at[h, i], g2_sem.at[h, g], along(h, d))
    for h in (0, 1):
        for q in range(1, n):
            wait(g1_sem.at[h, q, 0], hidden[0].at[h, 0, 0])
    result = jnp.zeros((8 * m, 256), F32)
    for g, (a, b) in enumerate(groups):
        for h in (0, 1):
            wait(g2_sem.at[h, g, 1], hidden[g].at[h, pl.ds(0, n - 1)])
            left = jnp.concatenate([hidden[g][h, :, k].reshape(8 * m, 128) for k in range(b - a)], axis=1)
            result += jnp.dot(left, down_w[(h * n + a) * 128 : (h * n + b) * 128, :], preferred_element_type=F32)

    pieces = result.reshape(m, 8, 256)
    last[...] = jnp.concatenate([pieces[:, :, :128], pieces[:, :, 128:]], axis=1).astype(BF16)
    for d in by_distance:
        send(last.at[lax.rem(gy + d, m)], got3.at[d - 1], f_sem, along_gy(d))
    for g in range(len(groups)):
        for h in (0, 1):
            wait(g2_sem.at[h, g, 0], hidden[g].at[h, pl.ds(0, n - 1)])
    acc = last[gy].astype(F32)
    wait(f_sem.at[1], got3)
    acc += jnp.sum(got3[...].astype(F32), axis=0)
    out_ref[...] = (jnp.concatenate([acc[:8], acc[8:]], axis=1) * down_s[...]).astype(BF16)
    wait(f_sem.at[0], got3)


def solution(mesh):
    n = int(round(mesh.shape["gx"] ** 0.5))
    m = mesh.shape["gy"]
    chunks, groups = cut(n, CHUNKS), cut(n, GROUPS)
    ahead, behind, direct = routes(n)
    relays = len(ahead) + len(behind)
    arrivals = len(direct) + (2 if relays else 0)
    half = 128 * n
    dma = pltpu.SemaphoreType.DMA

    def local(tokens, gate_weight, up_weight, gate_scale, up_scale, down_weight, down_scale):
        return pl.pallas_call(
            functools.partial(kernel, n, m, chunks, groups),
            out_shape=pltpu.VMEM((8, 256), BF16),
            in_specs=[pl.BlockSpec(memory_space=pltpu.HBM)] * 7,
            out_specs=pl.BlockSpec(memory_space=pltpu.VMEM),
            scratch_shapes=[
                pltpu.VMEM((8, 256), BF16),
                pltpu.VMEM((2, 256, 2 * half), BF16),
                pltpu.VMEM((2 * n, 128), F32),
                pltpu.VMEM((2 * n, 128), F32),
                pltpu.VMEM((2 * half, 256), BF16),
                pltpu.VMEM((1, 256), F32),
                pltpu.VMEM((16, 128), BF16),
                pltpu.VMEM((m, 16, 128), BF16),
                *[pltpu.VMEM((2, n, 16, (b - a) * 256), BF16) for a, b in chunks],
                *[pltpu.VMEM((2, arrivals, 16, (b - a) * 256), BF16) for a, b in chunks],
                *[pltpu.VMEM((2, max(1, relays), 16, (b - a) * 256), BF16) for a, b in chunks],
                *[pltpu.VMEM((2, 2, 16, (b - a) * 256), BF16) for a, b in chunks],
                pltpu.VMEM((2, n, 16, 256), BF16),
                pltpu.VMEM((2, n - 1, 16, 256), BF16),
                *[pltpu.VMEM((2, n, b - a, 16, 128), BF16) for a, b in groups],
                pltpu.VMEM((m, 16, 128), BF16),
                pltpu.VMEM((m - 1, 16, 128), BF16),
                dma((6,)),
                dma((2,)),
                dma((2, len(chunks), 2)),
                dma((2, len(chunks), 2)),
                dma((2, 2)),
                dma((2, n, 2)),
                dma((2, len(groups), 2)),
                dma((2,)),
            ],
            compiler_params=pltpu.CompilerParams(
                collective_id=0, has_side_effects=True, vmem_limit_bytes=60 << 20
            ),
            name="feed_forward",
        )(
            tokens,
            gate_weight,
            up_weight,
            gate_scale.reshape(2 * n, 128),
            up_scale.reshape(2 * n, 128),
            down_weight,
            down_scale.reshape(1, 256),
        )

    return jax.shard_map(
        local,
        mesh=mesh,
        in_specs=(P("gy", "gx"), P("gx", "gy"), P("gx", "gy"), P("gy"), P("gy"), P("gy", "gx"), P("gx")),
        out_specs=P("gy", "gx"),
        check_vma=False,
    )
```

```python
import functools

import jax
import jax.numpy as jnp
from jax import lax
from jax.experimental import pallas as pl
from jax.experimental.pallas import tpu as pltpu
from jax.sharding import PartitionSpec as P

MESH = pl.DeviceIdType.MESH
F32, BF16 = jnp.float32, jnp.bfloat16


def far_first(n):
    return sorted(range(1, n), key=lambda d: -min(d, n - d))


def routes(n):
    if n == 8:
        return [(-4, -2), (-3, -1)], [(3, 1)], [-1, 1]
    return [], [], list(range(1, n))


def by_hops(n):
    return [(0, 1)] + [(2 * k - 1, min(2 * k + 1, n)) for k in range(1, n // 2 + 1)]


def cut(n, parts):
    return [(n * k // parts, n * (k + 1) // parts) for k in range(parts)]


CHUNKS = 4


def kernel(n, m, chunks, groups, tokens_hbm, gate_hbm, up_hbm, gate_scale_hbm, up_scale_hbm, down_hbm, down_scale_hbm, out_ref,
           tokens_own, weights, gate_s, up_s, down_w, down_s, packed, gathered, *rest):
    parts, rest = rest[: len(chunks)], rest[len(chunks) :]
    got1, rest = rest[: len(chunks)], rest[len(chunks) :]
    relayed, rest = rest[: len(chunks)], rest[len(chunks) :]
    passed, rest = rest[: len(chunks)], rest[len(chunks) :]
    sums1, got2 = rest[:2]
    hidden, rest = rest[2 : 2 + len(groups)], rest[2 + len(groups) :]
    last, got3, load_sem, tok_sem, rl_sem, r1_sem, r2_sem, g1_sem, g2_sem, f_sem = rest
    gx, gy = lax.axis_index("gx"), lax.axis_index("gy")
    z, y = gx // n, lax.rem(gx, n)
    to_send = far_first(n) + [0]
    to_keep = to_send[::-1]

    def place(q):
        for g, (a, b) in enumerate(groups):
            if a <= q < b:
                return g, q - a

    def along(axis, d):
        if axis == 0:
            return (z * n + lax.rem(y + d, n), gy)
        return (lax.rem(z + d, n) * n + y, gy)

    def along_gy(d):
        return (gx, lax.rem(gy + d, m))

    side = 1 - 2 * lax.rem(gy, 2)

    def turned(d):
        return lax.rem(side * d + 2 * n, n)

    def where(axis, d):
        return lax.rem((y if axis == 0 else z) + d, n)

    def send(src, dst, sems, to):
        pltpu.make_async_remote_copy(
            src_ref=src, dst_ref=dst, send_sem=sems.at[0], recv_sem=sems.at[1], device_id=to, device_id_type=MESH
        ).start()

    def wait(sem, like):
        pltpu.make_async_copy(like, like, sem).wait()

    barrier = pltpu.get_barrier_semaphore()
    load_tokens = pltpu.make_async_copy(tokens_hbm, tokens_own, load_sem.at[0])
    load_tokens.start()
    by_distance = sorted(range(1, m), key=lambda d: -min(d // 2, n - d // 2))
    for d in by_distance:
        pl.semaphore_signal(barrier, inc=1, device_id=along_gy(d), device_id_type=MESH)
    for d in far_first(n):
        for axis in (0, 1):
            pl.semaphore_signal(barrier, inc=1, device_id=along(axis, d), device_id_type=MESH)

    for h in (0, 1):
        for p, e in enumerate(to_send):
            block = pl.ds(pl.multiple_of((h * n + where(1 - h, e)) * 128, 128), 128)
            pltpu.make_async_copy(gate_hbm.at[:, block], weights.at[h, :, pl.ds(p * 256, 128)], load_sem.at[1]).start()
            pltpu.make_async_copy(up_hbm.at[:, block], weights.at[h, :, pl.ds(p * 256 + 128, 128)], load_sem.at[1]).start()

    load_tokens.wait()
    own = tokens_own[...].astype(F32)
    packed[...] = jnp.concatenate([own[:, :128], own[:, 128:]], axis=0).astype(BF16)
    gathered[gy] = packed[...]
    pl.semaphore_wait(barrier, m - 1 + 2 * (n - 1))
    for d in by_distance:
        send(packed, gathered.at[gy], tok_sem, along_gy(d))
    for h in (0, 1):
        for q, e in enumerate(to_keep):
            block = pl.ds(pl.multiple_of((h * n + where(1 - h, e)) * 128, 128), 128)
            pltpu.make_async_copy(down_hbm.at[block, :], down_w.at[pl.ds((h * n + q) * 128, 128), :], load_sem.at[2]).start()
    small = [
        pltpu.make_async_copy(a, b, load_sem.at[3 + k])
        for k, (a, b) in enumerate(((gate_scale_hbm, gate_s), (up_scale_hbm, up_s), (down_scale_hbm, down_s)))
    ]
    for load in small:
        load.start()
    wait(load_sem.at[1], weights)
    wait(tok_sem.at[1], gathered.at[pl.ds(0, m - 1)])
    wide = gathered[...].astype(F32)
    x = jnp.concatenate([wide[:, :8].reshape(8 * m, 128), wide[:, 8:].reshape(8 * m, 128)], axis=1).astype(BF16)

    ahead, behind, direct = routes(n)
    for c, (a, b) in enumerate(chunks):
        for h in (0, 1):
            sums = jnp.dot(x, weights[h, :, a * 256 : b * 256], preferred_element_type=F32)
            parts[c][h] = sums.astype(BF16).reshape(n, 16, (b - a) * 256)
            for s, (far, stop) in enumerate(ahead + behind):
                send(parts[c].at[h, where(h, turned(far))], relayed[c].at[h, s], rl_sem.at[h, c], along(h, turned(stop)))
    for c in range(len(chunks)):
        for h in (0, 1):
            for s, d in enumerate(direct):
                send(parts[c].at[h, where(h, turned(d))], got1[c].at[h, s], r1_sem.at[h, c], along(h, turned(d)))
    wait(tok_sem.at[0], gathered.at[pl.ds(0, m - 1)])
    for load in small:
        load.wait()
    wait(load_sem.at[2], down_w)
    for c in range(len(chunks)):
        for h in (0, 1):
            if ahead:
                wait(rl_sem.at[h, c, 1], relayed[c].at[h])
                for s, (d, first, count) in enumerate(((-2, 0, len(ahead)), (2, len(ahead), len(behind)))):
                    acc = parts[c][h, where(h, turned(d))].astype(F32)
                    for k in range(first, first + count):
                        acc += relayed[c][h, k].astype(F32)
                    passed[c][h, s] = acc.astype(BF16)
                    send(passed[c].at[h, s], got1[c].at[h, len(direct) + s], r1_sem.at[h, c], along(h, turned(d)))
    for c, (a, b) in enumerate(chunks):
        for h in (0, 1):
            wait(r1_sem.at[h, c, 1], got1[c].at[h])
            acc = parts[c][h, where(h, 0)].astype(F32)
            for k in range(got1[c].shape[1]):
                acc += got1[c][h, k].astype(F32)
            for p in range(a, b):
                sums1[h, p] = acc[:, (p - a) * 256 : (p - a + 1) * 256].astype(BF16)
            for p in range(a, b):
                if to_send[p]:
                    send(sums1.at[h, p], got2.at[h, p], r2_sem.at[h], along(1 - h, to_send[p]))

    for c in range(len(chunks)):
        for h in (0, 1):
            wait(r1_sem.at[h, c, 0], got1[c].at[h])
            if ahead:
                wait(rl_sem.at[h, c, 0], relayed[c].at[h])
    for h in (0, 1):
        i, j = where(h, 0), where(1 - h, 0)
        wait(r2_sem.at[h, 1], got2.at[h])
        acc = sums1[h, n - 1].astype(F32)
        for p in range(n - 1):
            acc += got2[h, p].astype(F32)
        gate = acc[:, :128] * gate_s[pl.ds(h * n + j, 1), :]
        up = acc[:, 128:] * up_s[pl.ds(h * n + j, 1), :]
        hidden[0][h, i, 0] = (gate / (1.0 + jnp.exp(-gate)) * up).astype(BF16)
        for f in far_first(n):
            g, k = place(to_keep.index(n - f))
            send(hidden[0].at[h, i, 0], hidden[g].at[h, i, k], g1_sem.at[h, to_keep.index(n - f)], along(1 - h, f))
    for h in (0, 1):
        wait(r2_sem.at[h, 0], got2.at[h])
    for g, (a, b) in enumerate(groups):
        for h in (0, 1):
            i = where(h, 0)
            for q in range(max(a, 1), b):
                wait(g1_sem.at[h, q, 1], hidden[g].at[h, i, q - a])
            for d in far_first(n):
                send(hidden[g].at[h, i], hidden[g].at[h, i], g2_sem.at[h, g], along(h, d))
    for h in (0, 1):
        for q in range(1, n):
            wait(g1_sem.at[h, q, 0], hidden[0].at[h, 0, 0])
    result = jnp.zeros((8 * m, 256), F32)
    for g, (a, b) in enumerate(groups):
        for h in (0, 1):
            wait(g2_sem.at[h, g, 1], hidden[g].at[h, pl.ds(0, n - 1)])
            left = jnp.concatenate([hidden[g][h, :, k].reshape(8 * m, 128) for k in range(b - a)], axis=1)
            result += jnp.dot(left, down_w[(h * n + a) * 128 : (h * n + b) * 128, :], preferred_element_type=F32)

    pieces = result.reshape(m, 8, 256)
    last[...] = jnp.concatenate([pieces[:, :, :128], pieces[:, :, 128:]], axis=1).astype(BF16)
    for d in by_distance:
        send(last.at[lax.rem(gy + d, m)], got3.at[d - 1], f_sem, along_gy(d))
    for g in range(len(groups)):
        for h in (0, 1):
            wait(g2_sem.at[h, g, 0], hidden[g].at[h, pl.ds(0, n - 1)])
    acc = last[gy].astype(F32)
    wait(f_sem.at[1], got3)
    acc += jnp.sum(got3[...].astype(F32), axis=0)
    out_ref[...] = (jnp.concatenate([acc[:8], acc[8:]], axis=1) * down_s[...]).astype(BF16)
    wait(f_sem.at[0], got3)


def solution(mesh):
    n = int(round(mesh.shape["gx"] ** 0.5))
    m = mesh.shape["gy"]
    chunks, groups = cut(n, min(n, CHUNKS)), by_hops(n)
    ahead, behind, direct = routes(n)
    relays = len(ahead) + len(behind)
    arrivals = len(direct) + (2 if relays else 0)
    half = 128 * n
    dma = pltpu.SemaphoreType.DMA

    def local(tokens, gate_weight, up_weight, gate_scale, up_scale, down_weight, down_scale):
        return pl.pallas_call(
            functools.partial(kernel, n, m, chunks, groups),
            out_shape=pltpu.VMEM((8, 256), BF16),
            in_specs=[pl.BlockSpec(memory_space=pltpu.HBM)] * 7,
            out_specs=pl.BlockSpec(memory_space=pltpu.VMEM),
            scratch_shapes=[
                pltpu.VMEM((8, 256), BF16),
                pltpu.VMEM((2, 256, 2 * half), BF16),
                pltpu.VMEM((2 * n, 128), F32),
                pltpu.VMEM((2 * n, 128), F32),
                pltpu.VMEM((2 * half, 256), BF16),
                pltpu.VMEM((1, 256), F32),
                pltpu.VMEM((16, 128), BF16),
                pltpu.VMEM((m, 16, 128), BF16),
                *[pltpu.VMEM((2, n, 16, (b - a) * 256), BF16) for a, b in chunks],
                *[pltpu.VMEM((2, arrivals, 16, (b - a) * 256), BF16) for a, b in chunks],
                *[pltpu.VMEM((2, max(1, relays), 16, (b - a) * 256), BF16) for a, b in chunks],
                *[pltpu.VMEM((2, 2, 16, (b - a) * 256), BF16) for a, b in chunks],
                pltpu.VMEM((2, n, 16, 256), BF16),
                pltpu.VMEM((2, n - 1, 16, 256), BF16),
                *[pltpu.VMEM((2, n, b - a, 16, 128), BF16) for a, b in groups],
                pltpu.VMEM((m, 16, 128), BF16),
                pltpu.VMEM((m - 1, 16, 128), BF16),
                dma((6,)),
                dma((2,)),
                dma((2, len(chunks), 2)),
                dma((2, len(chunks), 2)),
                dma((2, 2)),
                dma((2, n, 2)),
                dma((2, len(groups), 2)),
                dma((2,)),
            ],
            compiler_params=pltpu.CompilerParams(
                collective_id=0, has_side_effects=True, vmem_limit_bytes=60 << 20
            ),
            name="feed_forward",
        )(
            tokens,
            gate_weight,
            up_weight,
            gate_scale.reshape(2 * n, 128),
            up_scale.reshape(2 * n, 128),
            down_weight,
            down_scale.reshape(1, 256),
        )

    return jax.shard_map(
        local,
        mesh=mesh,
        in_specs=(P("gy", "gx"), P("gx", "gy"), P("gx", "gy"), P("gy"), P("gy"), P("gy", "gx"), P("gx")),
        out_specs=P("gy", "gx"),
        check_vma=False,
    )
```

```python
import functools

import jax
import jax.numpy as jnp
from jax import lax
from jax.experimental import pallas as pl
from jax.experimental.pallas import tpu as pltpu
from jax.sharding import PartitionSpec as P

MESH = pl.DeviceIdType.MESH
F32, BF16 = jnp.float32, jnp.bfloat16


def far_first(n):
    return sorted(range(1, n), key=lambda d: -min(d, n - d))


def routes(n):
    if n == 8:
        return [(-4, -2), (-3, -1)], [(3, 1)], [-1, 1]
    return [], [], list(range(1, n))


def by_hops(n):
    return [(0, 1)] + [(2 * k - 1, min(2 * k + 1, n)) for k in range(1, n // 2 + 1)]


def cut(n, parts):
    return [(n * k // parts, n * (k + 1) // parts) for k in range(parts)]


CHUNKS = 4


def kernel(n, m, chunks, groups, tokens_hbm, gate_hbm, up_hbm, gate_scale_hbm, up_scale_hbm, down_hbm, down_scale_hbm, out_ref,
           tokens_own, weights, gate_s, up_s, down_w, down_s, packed, gathered, *rest):
    parts, rest = rest[: len(chunks)], rest[len(chunks) :]
    got1, rest = rest[: len(chunks)], rest[len(chunks) :]
    relayed, rest = rest[: len(chunks)], rest[len(chunks) :]
    passed, rest = rest[: len(chunks)], rest[len(chunks) :]
    sums1, got2 = rest[:2]
    hidden, rest = rest[2 : 2 + len(groups)], rest[2 + len(groups) :]
    last, got3, load_sem, tok_sem, rl_sem, r1_sem, r2_sem, g1_sem, g2_sem, f_sem, here_sem = rest
    gx, gy = lax.axis_index("gx"), lax.axis_index("gy")
    z, y = gx // n, lax.rem(gx, n)
    to_send = far_first(n) + [0]
    to_keep = to_send[::-1]

    def place(q):
        for g, (a, b) in enumerate(groups):
            if a <= q < b:
                return g, q - a

    def along(axis, d):
        if axis == 0:
            return (z * n + lax.rem(y + d, n), gy)
        return (lax.rem(z + d, n) * n + y, gy)

    def along_gy(d):
        return (gx, lax.rem(gy + d, m))

    side = 1 - 2 * lax.rem(gy, 2)

    def turned(d):
        return lax.rem(side * d + 2 * n, n)

    def where(axis, d):
        return lax.rem((y if axis == 0 else z) + d, n)

    def send(src, dst, sems, to):
        pltpu.make_async_remote_copy(
            src_ref=src, dst_ref=dst, send_sem=sems.at[0], recv_sem=sems.at[1], device_id=to, device_id_type=MESH
        ).start()

    def wait(sem, like):
        pltpu.make_async_copy(like, like, sem).wait()

    barrier = pltpu.get_barrier_semaphore()
    load_tokens = pltpu.make_async_copy(tokens_hbm, tokens_own, load_sem.at[0])
    load_tokens.start()
    by_distance = sorted(range(1, m), key=lambda d: -min(d // 2, n - d // 2))
    for d in by_distance:
        pl.semaphore_signal(barrier, inc=1, device_id=along_gy(d), device_id_type=MESH)
    def order(axis, d):
        i = where(axis, d)
        return i if axis else jnp.where(i < n // 2, i, n + n // 2 - 1 - i)

    before = order(0, 0) + order(1, 0)
    after = 2 * (n - 1) - before
    for d in far_first(n):
        for axis in (0, 1):

            @pl.when(order(axis, d) > order(axis, 0))
            def _():
                pl.semaphore_signal(barrier, inc=1, device_id=along(axis, d), device_id_type=MESH)


    for h in (0, 1):
        for p, e in enumerate(to_send):
            block = pl.ds(pl.multiple_of((h * n + where(1 - h, e)) * 128, 128), 128)
            pltpu.make_async_copy(gate_hbm.at[:, block], weights.at[h, :, pl.ds(p * 256, 128)], load_sem.at[1]).start()
            pltpu.make_async_copy(up_hbm.at[:, block], weights.at[h, :, pl.ds(p * 256 + 128, 128)], load_sem.at[1]).start()

    load_tokens.wait()
    own = tokens_own[...].astype(F32)
    packed[...] = jnp.concatenate([own[:, :128], own[:, 128:]], axis=0).astype(BF16)
    gathered[gy] = packed[...]
    pl.semaphore_wait(barrier, m - 1 + before)
    for d in by_distance:
        send(packed, gathered.at[gy], tok_sem, along_gy(d))
    for d in far_first(n):
        for axis in (0, 1):

            @pl.when(order(axis, d) < order(axis, 0))
            def _():
                pl.semaphore_signal(here_sem, inc=1, device_id=along(axis, d), device_id_type=MESH)

    for h in (0, 1):
        for q, e in enumerate(to_keep):
            block = pl.ds(pl.multiple_of((h * n + where(1 - h, e)) * 128, 128), 128)
            pltpu.make_async_copy(down_hbm.at[block, :], down_w.at[pl.ds((h * n + q) * 128, 128), :], load_sem.at[2]).start()
    small = [
        pltpu.make_async_copy(a, b, load_sem.at[3 + k])
        for k, (a, b) in enumerate(((gate_scale_hbm, gate_s), (up_scale_hbm, up_s), (down_scale_hbm, down_s)))
    ]
    for load in small:
        load.start()
    wait(load_sem.at[1], weights)
    wait(tok_sem.at[1], gathered.at[pl.ds(0, m - 1)])
    wide = gathered[...].astype(F32)
    x = jnp.concatenate([wide[:, :8].reshape(8 * m, 128), wide[:, 8:].reshape(8 * m, 128)], axis=1).astype(BF16)

    @pl.when(after > 0)
    def _():
        pl.semaphore_wait(here_sem, after)

    ahead, behind, direct = routes(n)
    for c, (a, b) in enumerate(chunks):
        for h in (0, 1):
            sums = jnp.dot(x, weights[h, :, a * 256 : b * 256], preferred_element_type=F32)
            parts[c][h] = sums.astype(BF16).reshape(n, 16, (b - a) * 256)
            for s, (far, stop) in enumerate(ahead + behind):
                send(parts[c].at[h, where(h, turned(far))], relayed[c].at[h, s], rl_sem.at[h, c], along(h, turned(stop)))
    for c in range(len(chunks)):
        for h in (0, 1):
            for s, d in enumerate(direct):
                send(parts[c].at[h, where(h, turned(d))], got1[c].at[h, s], r1_sem.at[h, c], along(h, turned(d)))
    wait(tok_sem.at[0], gathered.at[pl.ds(0, m - 1)])
    for load in small:
        load.wait()
    wait(load_sem.at[2], down_w)
    for c in range(len(chunks)):
        for h in (0, 1):
            if ahead:
                wait(rl_sem.at[h, c, 1], relayed[c].at[h])
                for s, (d, first, count) in enumerate(((-2, 0, len(ahead)), (2, len(ahead), len(behind)))):
                    acc = parts[c][h, where(h, turned(d))].astype(F32)
                    for k in range(first, first + count):
                        acc += relayed[c][h, k].astype(F32)
                    passed[c][h, s] = acc.astype(BF16)
                    send(passed[c].at[h, s], got1[c].at[h, len(direct) + s], r1_sem.at[h, c], along(h, turned(d)))
    for c, (a, b) in enumerate(chunks):
        for h in (0, 1):
            wait(r1_sem.at[h, c, 1], got1[c].at[h])
            acc = parts[c][h, where(h, 0)].astype(F32)
            for k in range(got1[c].shape[1]):
                acc += got1[c][h, k].astype(F32)
            for p in range(a, b):
                sums1[h, p] = acc[:, (p - a) * 256 : (p - a + 1) * 256].astype(BF16)
            for p in range(a, b):
                if to_send[p]:
                    send(sums1.at[h, p], got2.at[h, p], r2_sem.at[h], along(1 - h, to_send[p]))

    for c in range(len(chunks)):
        for h in (0, 1):
            wait(r1_sem.at[h, c, 0], got1[c].at[h])
            if ahead:
                wait(rl_sem.at[h, c, 0], relayed[c].at[h])
    for h in (0, 1):
        i, j = where(h, 0), where(1 - h, 0)
        wait(r2_sem.at[h, 1], got2.at[h])
        acc = sums1[h, n - 1].astype(F32)
        for p in range(n - 1):
            acc += got2[h, p].astype(F32)
        gate = acc[:, :128] * gate_s[pl.ds(h * n + j, 1), :]
        up = acc[:, 128:] * up_s[pl.ds(h * n + j, 1), :]
        hidden[0][h, i, 0] = (gate / (1.0 + jnp.exp(-gate)) * up).astype(BF16)
        for f in far_first(n):
            g, k = place(to_keep.index(n - f))
            send(hidden[0].at[h, i, 0], hidden[g].at[h, i, k], g1_sem.at[h, to_keep.index(n - f)], along(1 - h, f))
    for h in (0, 1):
        wait(r2_sem.at[h, 0], got2.at[h])
    for g, (a, b) in enumerate(groups):
        for h in (0, 1):
            i = where(h, 0)
            for q in range(max(a, 1), b):
                wait(g1_sem.at[h, q, 1], hidden[g].at[h, i, q - a])
            for d in far_first(n):
                send(hidden[g].at[h, i], hidden[g].at[h, i], g2_sem.at[h, g], along(h, d))
    for h in (0, 1):
        for q in range(1, n):
            wait(g1_sem.at[h, q, 0], hidden[0].at[h, 0, 0])
    result = jnp.zeros((8 * m, 256), F32)
    for g, (a, b) in enumerate(groups):
        for h in (0, 1):
            wait(g2_sem.at[h, g, 1], hidden[g].at[h, pl.ds(0, n - 1)])
            left = jnp.concatenate([hidden[g][h, :, k].reshape(8 * m, 128) for k in range(b - a)], axis=1)
            result += jnp.dot(left, down_w[(h * n + a) * 128 : (h * n + b) * 128, :], preferred_element_type=F32)

    pieces = result.reshape(m, 8, 256)
    last[...] = jnp.concatenate([pieces[:, :, :128], pieces[:, :, 128:]], axis=1).astype(BF16)
    for d in by_distance:
        send(last.at[lax.rem(gy + d, m)], got3.at[d - 1], f_sem, along_gy(d))
    for g in range(len(groups)):
        for h in (0, 1):
            wait(g2_sem.at[h, g, 0], hidden[g].at[h, pl.ds(0, n - 1)])
    acc = last[gy].astype(F32)
    wait(f_sem.at[1], got3)
    acc += jnp.sum(got3[...].astype(F32), axis=0)
    out_ref[...] = (jnp.concatenate([acc[:8], acc[8:]], axis=1) * down_s[...]).astype(BF16)
    wait(f_sem.at[0], got3)


def solution(mesh):
    n = int(round(mesh.shape["gx"] ** 0.5))
    m = mesh.shape["gy"]
    chunks, groups = cut(n, min(n, CHUNKS)), by_hops(n)
    ahead, behind, direct = routes(n)
    relays = len(ahead) + len(behind)
    arrivals = len(direct) + (2 if relays else 0)
    half = 128 * n
    dma = pltpu.SemaphoreType.DMA

    def local(tokens, gate_weight, up_weight, gate_scale, up_scale, down_weight, down_scale):
        return pl.pallas_call(
            functools.partial(kernel, n, m, chunks, groups),
            out_shape=pltpu.VMEM((8, 256), BF16),
            in_specs=[pl.BlockSpec(memory_space=pltpu.HBM)] * 7,
            out_specs=pl.BlockSpec(memory_space=pltpu.VMEM),
            scratch_shapes=[
                pltpu.VMEM((8, 256), BF16),
                pltpu.VMEM((2, 256, 2 * half), BF16),
                pltpu.VMEM((2 * n, 128), F32),
                pltpu.VMEM((2 * n, 128), F32),
                pltpu.VMEM((2 * half, 256), BF16),
                pltpu.VMEM((1, 256), F32),
                pltpu.VMEM((16, 128), BF16),
                pltpu.VMEM((m, 16, 128), BF16),
                *[pltpu.VMEM((2, n, 16, (b - a) * 256), BF16) for a, b in chunks],
                *[pltpu.VMEM((2, arrivals, 16, (b - a) * 256), BF16) for a, b in chunks],
                *[pltpu.VMEM((2, max(1, relays), 16, (b - a) * 256), BF16) for a, b in chunks],
                *[pltpu.VMEM((2, 2, 16, (b - a) * 256), BF16) for a, b in chunks],
                pltpu.VMEM((2, n, 16, 256), BF16),
                pltpu.VMEM((2, n - 1, 16, 256), BF16),
                *[pltpu.VMEM((2, n, b - a, 16, 128), BF16) for a, b in groups],
                pltpu.VMEM((m, 16, 128), BF16),
                pltpu.VMEM((m - 1, 16, 128), BF16),
                dma((6,)),
                dma((2,)),
                dma((2, len(chunks), 2)),
                dma((2, len(chunks), 2)),
                dma((2, 2)),
                dma((2, n, 2)),
                dma((2, len(groups), 2)),
                dma((2,)),
                pltpu.SemaphoreType.REGULAR,
            ],
            compiler_params=pltpu.CompilerParams(
                collective_id=0, has_side_effects=True, vmem_limit_bytes=60 << 20
            ),
            name="feed_forward",
        )(
            tokens,
            gate_weight,
            up_weight,
            gate_scale.reshape(2 * n, 128),
            up_scale.reshape(2 * n, 128),
            down_weight,
            down_scale.reshape(1, 256),
        )

    return jax.shard_map(
        local,
        mesh=mesh,
        in_specs=(P("gy", "gx"), P("gx", "gy"), P("gx", "gy"), P("gy"), P("gy"), P("gy", "gx"), P("gx")),
        out_specs=P("gy", "gx"),
        check_vma=False,
    )
```

```python
import functools

import jax
import jax.numpy as jnp
from jax import lax
from jax.experimental import pallas as pl
from jax.experimental.pallas import tpu as pltpu
from jax.sharding import PartitionSpec as P

MESH = pl.DeviceIdType.MESH
F32, BF16 = jnp.float32, jnp.bfloat16


def far_first(n):
    return sorted(range(1, n), key=lambda d: -min(d, n - d))


def routes(n):
    if n == 8:
        return [(-4, -2), (-3, -1)], [(3, 1)], [-1, 1]
    return [], [], list(range(1, n))


def by_hops(n):
    return [(0, 1)] + [(2 * k - 1, min(2 * k + 1, n)) for k in range(1, n // 2 + 1)]


def cut(n, parts):
    return [(n * k // parts, n * (k + 1) // parts) for k in range(parts)]


CHUNKS = 3


def kernel(n, m, chunks, groups, tokens_hbm, gate_hbm, up_hbm, gate_scale_hbm, up_scale_hbm, down_hbm, down_scale_hbm, out_ref,
           tokens_own, weights, gate_s, up_s, down_w, down_s, packed, gathered, *rest):
    parts, rest = rest[: len(chunks)], rest[len(chunks) :]
    got1, rest = rest[: len(chunks)], rest[len(chunks) :]
    relayed, rest = rest[: len(chunks)], rest[len(chunks) :]
    passed, rest = rest[: len(chunks)], rest[len(chunks) :]
    sums1, got2 = rest[:2]
    hidden, rest = rest[2 : 2 + len(groups)], rest[2 + len(groups) :]
    last, got3, load_sem, tok_sem, rl_sem, r1_sem, r2_sem, g1_sem, g2_sem, f_sem = rest
    gx, gy = lax.axis_index("gx"), lax.axis_index("gy")
    z, y = gx // n, lax.rem(gx, n)
    to_send = far_first(n) + [0]
    to_keep = to_send[::-1]

    def place(q):
        for g, (a, b) in enumerate(groups):
            if a <= q < b:
                return g, q - a

    def along(axis, d):
        if axis == 0:
            return (z * n + lax.rem(y + d, n), gy)
        return (lax.rem(z + d, n) * n + y, gy)

    def along_gy(d):
        return (gx, lax.rem(gy + d, m))

    side = 1 - 2 * lax.rem(gy, 2)

    def turned(d):
        return lax.rem(side * d + 2 * n, n)

    def where(axis, d):
        return lax.rem((y if axis == 0 else z) + d, n)

    def send(src, dst, sems, to):
        pltpu.make_async_remote_copy(
            src_ref=src, dst_ref=dst, send_sem=sems.at[0], recv_sem=sems.at[1], device_id=to, device_id_type=MESH
        ).start()

    def wait(sem, like):
        pltpu.make_async_copy(like, like, sem).wait()

    barrier = pltpu.get_barrier_semaphore()
    load_tokens = pltpu.make_async_copy(tokens_hbm, tokens_own, load_sem.at[0])
    load_tokens.start()
    by_distance = sorted(range(1, m), key=lambda d: -min(d // 2, n - d // 2))
    for d in by_distance:
        pl.semaphore_signal(barrier, inc=1, device_id=along_gy(d), device_id_type=MESH)
    for d in far_first(n):
        for axis in (0, 1):
            pl.semaphore_signal(barrier, inc=1, device_id=along(axis, d), device_id_type=MESH)

    load_tokens.wait()
    own = tokens_own[...].astype(F32)
    packed[...] = jnp.concatenate([own[:, :128], own[:, 128:]], axis=0).astype(BF16)
    gathered[gy] = packed[...]
    pl.semaphore_wait(barrier, m - 1 + 2 * (n - 1))
    for d in by_distance:
        send(packed, gathered.at[gy], tok_sem, along_gy(d))

    for h in (0, 1):
        for p, e in enumerate(to_send):
            block = pl.ds(pl.multiple_of((h * n + where(1 - h, e)) * 128, 128), 128)
            pltpu.make_async_copy(gate_hbm.at[:, block], weights.at[h, :, pl.ds(p * 256, 128)], load_sem.at[1]).start()
            pltpu.make_async_copy(up_hbm.at[:, block], weights.at[h, :, pl.ds(p * 256 + 128, 128)], load_sem.at[1]).start()
    for h in (0, 1):
        for q, e in enumerate(to_keep):
            block = pl.ds(pl.multiple_of((h * n + where(1 - h, e)) * 128, 128), 128)
            pltpu.make_async_copy(down_hbm.at[block, :], down_w.at[pl.ds((h * n + q) * 128, 128), :], load_sem.at[2]).start()
    small = [
        pltpu.make_async_copy(a, b, load_sem.at[3 + k])
        for k, (a, b) in enumerate(((gate_scale_hbm, gate_s), (up_scale_hbm, up_s), (down_scale_hbm, down_s)))
    ]
    for load in small:
        load.start()
    wait(load_sem.at[1], weights)
    wait(tok_sem.at[1], gathered.at[pl.ds(0, m - 1)])
    wide = gathered[...].astype(F32)
    x = jnp.concatenate([wide[:, :8].reshape(8 * m, 128), wide[:, 8:].reshape(8 * m, 128)], axis=1).astype(BF16)

    ahead, behind, direct = routes(n)
    for c, (a, b) in enumerate(chunks):
        for h in (0, 1):
            sums = jnp.dot(x, weights[h, :, a * 256 : b * 256], preferred_element_type=F32)
            parts[c][h] = sums.astype(BF16).reshape(n, 16, (b - a) * 256)
            for s, (far, stop) in enumerate(ahead + behind):
                send(parts[c].at[h, where(h, turned(far))], relayed[c].at[h, s], rl_sem.at[h, c], along(h, turned(stop)))
    for c in range(len(chunks)):
        for h in (0, 1):
            for s, d in enumerate(direct):
                send(parts[c].at[h, where(h, turned(d))], got1[c].at[h, s], r1_sem.at[h, c], along(h, turned(d)))
    wait(tok_sem.at[0], gathered.at[pl.ds(0, m - 1)])
    for load in small:
        load.wait()
    wait(load_sem.at[2], down_w)
    for c in range(len(chunks)):
        for h in (0, 1):
            if ahead:
                wait(rl_sem.at[h, c, 1], relayed[c].at[h])
                for s, (d, first, count) in enumerate(((-2, 0, len(ahead)), (2, len(ahead), len(behind)))):
                    acc = parts[c][h, where(h, turned(d))].astype(F32)
                    for k in range(first, first + count):
                        acc += relayed[c][h, k].astype(F32)
                    passed[c][h, s] = acc.astype(BF16)
                    send(passed[c].at[h, s], got1[c].at[h, len(direct) + s], r1_sem.at[h, c], along(h, turned(d)))
    for c, (a, b) in enumerate(chunks):
        for h in (0, 1):
            wait(r1_sem.at[h, c, 1], got1[c].at[h])
            acc = parts[c][h, where(h, 0)].astype(F32)
            for k in range(got1[c].shape[1]):
                acc += got1[c][h, k].astype(F32)
            for p in range(a, b):
                sums1[h, p] = acc[:, (p - a) * 256 : (p - a + 1) * 256].astype(BF16)
            for p in range(a, b):
                if to_send[p]:
                    send(sums1.at[h, p], got2.at[h, p], r2_sem.at[h], along(1 - h, to_send[p]))

    for c in range(len(chunks)):
        for h in (0, 1):
            wait(r1_sem.at[h, c, 0], got1[c].at[h])
            if ahead:
                wait(rl_sem.at[h, c, 0], relayed[c].at[h])
    for h in (0, 1):
        i, j = where(h, 0), where(1 - h, 0)
        wait(r2_sem.at[h, 1], got2.at[h])
        acc = sums1[h, n - 1].astype(F32)
        for p in range(n - 1):
            acc += got2[h, p].astype(F32)
        gate = acc[:, :128] * gate_s[pl.ds(h * n + j, 1), :]
        up = acc[:, 128:] * up_s[pl.ds(h * n + j, 1), :]
        hidden[0][h, i, 0] = (gate / (1.0 + jnp.exp(-gate)) * up).astype(BF16)
        for f in far_first(n):
            g, k = place(to_keep.index(n - f))
            send(hidden[0].at[h, i, 0], hidden[g].at[h, i, k], g1_sem.at[h, to_keep.index(n - f)], along(1 - h, f))
    for h in (0, 1):
        wait(r2_sem.at[h, 0], got2.at[h])
    for g, (a, b) in enumerate(groups):
        for h in (0, 1):
            i = where(h, 0)
            for q in range(max(a, 1), b):
                wait(g1_sem.at[h, q, 1], hidden[g].at[h, i, q - a])
            for d in far_first(n):
                send(hidden[g].at[h, i], hidden[g].at[h, i], g2_sem.at[h, g], along(h, d))
    for h in (0, 1):
        for q in range(1, n):
            wait(g1_sem.at[h, q, 0], hidden[0].at[h, 0, 0])
    result = jnp.zeros((8 * m, 256), F32)
    for g, (a, b) in enumerate(groups):
        for h in (0, 1):
            wait(g2_sem.at[h, g, 1], hidden[g].at[h, pl.ds(0, n - 1)])
            left = jnp.concatenate([hidden[g][h, :, k].reshape(8 * m, 128) for k in range(b - a)], axis=1)
            result += jnp.dot(left, down_w[(h * n + a) * 128 : (h * n + b) * 128, :], preferred_element_type=F32)

    pieces = result.reshape(m, 8, 256)
    last[...] = jnp.concatenate([pieces[:, :, :128], pieces[:, :, 128:]], axis=1).astype(BF16)
    for d in by_distance:
        send(last.at[lax.rem(gy + d, m)], got3.at[d - 1], f_sem, along_gy(d))
    for g in range(len(groups)):
        for h in (0, 1):
            wait(g2_sem.at[h, g, 0], hidden[g].at[h, pl.ds(0, n - 1)])
    acc = last[gy].astype(F32)
    wait(f_sem.at[1], got3)
    acc += jnp.sum(got3[...].astype(F32), axis=0)
    out_ref[...] = (jnp.concatenate([acc[:8], acc[8:]], axis=1) * down_s[...]).astype(BF16)
    wait(f_sem.at[0], got3)


def solution(mesh):
    n = int(round(mesh.shape["gx"] ** 0.5))
    m = mesh.shape["gy"]
    chunks, groups = cut(n, min(n, CHUNKS)), by_hops(n)
    ahead, behind, direct = routes(n)
    relays = len(ahead) + len(behind)
    arrivals = len(direct) + (2 if relays else 0)
    half = 128 * n
    dma = pltpu.SemaphoreType.DMA

    def local(tokens, gate_weight, up_weight, gate_scale, up_scale, down_weight, down_scale):
        return pl.pallas_call(
            functools.partial(kernel, n, m, chunks, groups),
            out_shape=pltpu.VMEM((8, 256), BF16),
            in_specs=[pl.BlockSpec(memory_space=pltpu.HBM)] * 7,
            out_specs=pl.BlockSpec(memory_space=pltpu.VMEM),
            scratch_shapes=[
                pltpu.VMEM((8, 256), BF16),
                pltpu.VMEM((2, 256, 2 * half), BF16),
                pltpu.VMEM((2 * n, 128), F32),
                pltpu.VMEM((2 * n, 128), F32),
                pltpu.VMEM((2 * half, 256), BF16),
                pltpu.VMEM((1, 256), F32),
                pltpu.VMEM((16, 128), BF16),
                pltpu.VMEM((m, 16, 128), BF16),
                *[pltpu.VMEM((2, n, 16, (b - a) * 256), BF16) for a, b in chunks],
                *[pltpu.VMEM((2, arrivals, 16, (b - a) * 256), BF16) for a, b in chunks],
                *[pltpu.VMEM((2, max(1, relays), 16, (b - a) * 256), BF16) for a, b in chunks],
                *[pltpu.VMEM((2, 2, 16, (b - a) * 256), BF16) for a, b in chunks],
                pltpu.VMEM((2, n, 16, 256), BF16),
                pltpu.VMEM((2, n - 1, 16, 256), BF16),
                *[pltpu.VMEM((2, n, b - a, 16, 128), BF16) for a, b in groups],
                pltpu.VMEM((m, 16, 128), BF16),
                pltpu.VMEM((m - 1, 16, 128), BF16),
                dma((6,)),
                dma((2,)),
                dma((2, len(chunks), 2)),
                dma((2, len(chunks), 2)),
                dma((2, 2)),
                dma((2, n, 2)),
                dma((2, len(groups), 2)),
                dma((2,)),
            ],
            compiler_params=pltpu.CompilerParams(
                collective_id=0, has_side_effects=True, vmem_limit_bytes=60 << 20
            ),
            name="feed_forward",
        )(
            tokens,
            gate_weight,
            up_weight,
            gate_scale.reshape(2 * n, 128),
            up_scale.reshape(2 * n, 128),
            down_weight,
            down_scale.reshape(1, 256),
        )

    return jax.shard_map(
        local,
        mesh=mesh,
        in_specs=(P("gy", "gx"), P("gx", "gy"), P("gx", "gy"), P("gy"), P("gy"), P("gy", "gx"), P("gx")),
        out_specs=P("gy", "gx"),
        check_vma=False,
    )
```
